32 devices in a mesh: chan: 8 (over z, core), freq: 4 (over y, x).
Axes of the slice: x: 2, y: 2, z: 4, core: 2. Of those that a mesh axis runs over, the one named last changes fastest.
Arguments:
- records: bfloat16 [33792, 4096], P('freq', 'chan')
- offsets: int32 [256], P('freq'), may hold values from 0 to 8192, as said below
- dead_mask: int32 [4096], P('chan'), may hold values 0 or 1
- band_blocks: int32 [8], P('chan'), may hold values from 0 to 2, as said below
Outputs:
- cross: bfloat16 [3, 32, 4096, 1024], P(None, 'freq', 'chan')
The draws below stay inside these ranges and needn't reach their ends.
Inputs may be any that keep to these rules, and one draw needn't show every extreme that they name: offsets[s] is the first sample of segment s within time block s // 64 of 8448 samples; all 256 samples of the segment lie in that block. band_blocks[b] is the largest block offset whose cross-spectra are kept for channel block b.
All inputs are finite; a program needn't handle non-finite values. No bound on the sum of `dead_mask` on one device may be relied on, other than what follows from the above.
Results may differ from the reference program's by a relative error of at most 0.0055.
Values may be sent and summed in bfloat16 or wider, within the bound.
A program may use at most 128 MiB of HBM per device.

```python
import math
import jax
import jax.numpy as jnp
from jax import lax

CB = 512
SEG_LEN = 256
BINS = 32
FIRST_BIN = 2
BAND = 2
SEG_DEV = 64
SEGMENTS = 256
RECORD_DEV = 8448
TIME = 33792
NBLOCKS = 8
CHANNELS = 4096


def draw_records(key, part):
    noise_key, chan_key, time_key = jax.random.split(key, 3)
    window_count = TIME // (SEG_LEN // 2)
    noise_field = jax.random.normal(noise_key, (TIME, CHANNELS), jnp.float32)
    chan_scale = jnp.exp(jax.random.uniform(chan_key, (1, CHANNELS), jnp.float32, 0.0, math.log(10.0)))
    window_scale = jnp.exp(jax.random.uniform(time_key, (window_count,), jnp.float32, 0.0, math.log(10.0)))
    time_scale = jnp.repeat(window_scale, SEG_LEN // 2)[:, None]
    return (noise_field * chan_scale * time_scale).astype(jnp.bfloat16)


def draw_offsets(key, part):
    start_span = RECORD_DEV - SEG_LEN + 1
    values = jax.random.randint(key, (SEGMENTS,), 0, start_span, jnp.int32)
    chosen = jax.random.randint(jax.random.fold_in(key, 7), (2,), 0, SEGMENTS, jnp.int32)
    values = values.at[chosen[1]].set(0)
    values = values.at[chosen[0]].set(start_span - 1)
    return values


def draw_band_blocks(key, part):
    low_count = max(1, NBLOCKS // 2 - 2)
    narrow_block = jax.random.randint(jax.random.fold_in(key, 11), (), 0, low_count, jnp.int32)
    block_index = jnp.arange(NBLOCKS, dtype=jnp.int32)
    values = jnp.full((NBLOCKS,), BAND, jnp.int32)
    values = jnp.where(block_index == narrow_block, 0, values)
    values = jnp.where(block_index == narrow_block + 1, 1, values)
    return values.astype(jnp.int32)


def set_ends(result, own_key, smallest, largest):
    longest = result.shape.index(max(result.shape))
    spots = []
    for shift in (0, 1):
        where = [jax.random.randint(jax.random.fold_in(own_key, axis), (), 0, length) for axis, length in enumerate(result.shape)]
        where[longest] = (where[longest] + shift) % result.shape[longest]
        spots.append(tuple(where))
    return result.at[spots[0]].set(smallest).at[spots[1]].set(largest)


def setup_inputs(seed: int = 0) -> dict:
    keys = jax.random.split(jax.random.key(seed), 5)
    return {
        "records": draw_records(jax.random.fold_in(keys[4], 71), 0),
        "offsets": draw_offsets(jax.random.fold_in(keys[4], 71), 0),
        "dead_mask": set_ends((jax.random.randint(keys[2], (CHANNELS,), 0, 16) < 15).astype(jnp.int32), jax.random.fold_in(keys[2], 1), 0, 1),
        "band_blocks": draw_band_blocks(jax.random.fold_in(keys[4], 71), 0),
    }


EPS_POWER = 1e-06

def dft_table(seg_length, bin_count, first_bin):
    sample_index = jnp.arange(seg_length, dtype=jnp.int32)
    row_index = jnp.arange(2 * bin_count, dtype=jnp.int32)
    harmonic = row_index // 2 + first_bin
    phase_steps = harmonic[:, None] * sample_index[None, :] % seg_length
    phase_angle = 2.0 * jnp.pi / seg_length * phase_steps.astype(jnp.float32)
    hann_taper = 0.5 - 0.5 * jnp.cos(2.0 * jnp.pi / seg_length * sample_index.astype(jnp.float32))
    wave_rows = jnp.where((row_index % 2 == 0)[:, None], jnp.cos(phase_angle), -jnp.sin(phase_angle))
    return (hann_taper[None, :] * wave_rows).astype(jnp.bfloat16)

def reference(records, offsets, dead_mask, band_blocks):
    dft_rows = dft_table(SEG_LEN, BINS, FIRST_BIN)
    starts = jnp.arange(SEGMENTS, dtype=jnp.int32) // SEG_DEV * RECORD_DEV + offsets.astype(jnp.int32)
    live_mask = dead_mask.astype(jnp.float32)

    def one_segment(start_row):
        frame_rows = lax.dynamic_slice_in_dim(records, start_row, SEG_LEN, 0)
        spectra = jnp.dot(dft_rows, frame_rows, preferred_element_type=jnp.float32)
        band_power = lax.optimization_barrier(jnp.sum(spectra * spectra, axis=0)) * (1.0 / BINS)
        scaling = live_mask / jnp.sqrt(band_power + EPS_POWER)
        return (spectra * scaling[None, :]).astype(jnp.bfloat16)
    whitened = lax.map(one_segment, starts)
    panels = whitened.reshape(SEGMENTS, BINS, 2, CHANNELS).transpose(1, 2, 0, 3)
    panels = panels.reshape(BINS, 2 * SEGMENTS, NBLOCKS, CB)
    band_limit = band_blocks.astype(jnp.int32)

    def one_bin(bin_panel):
        left_panel = bin_panel.astype(jnp.float32)
        turned = jnp.concatenate([left_panel[SEGMENTS:], -left_panel[:SEGMENTS]], axis=0)
        outputs = []
        for offset_index in range(BAND + 1):
            right_panel = jnp.concatenate([left_panel[:, offset_index:], jnp.zeros((2 * SEGMENTS, offset_index, CB), jnp.float32)], axis=1)
            real_part = jnp.einsum('sbi,sbj->bij', left_panel, right_panel, precision=lax.Precision.HIGHEST)
            imag_part = jnp.einsum('sbi,sbj->bij', turned, right_panel, precision=lax.Precision.HIGHEST)
            cross_block = jnp.concatenate([real_part, imag_part], axis=2) * (1.0 / SEGMENTS)
            keep_flag = (offset_index <= band_limit).astype(jnp.bfloat16)
            outputs.append(cross_block.astype(jnp.bfloat16) * keep_flag[:, None, None])
        return jnp.stack(outputs, axis=0)
    per_bin = lax.map(one_bin, panels)
    return per_bin.transpose(1, 0, 2, 3, 4).reshape(BAND + 1, BINS, CHANNELS, 2 * CB)
```

```python
import functools

import jax
import jax.numpy as jnp
import ml_dtypes
import numpy as np
from jax import lax
from jax.experimental import pallas as pl
from jax.experimental.pallas import tpu as pltpu
from jax.sharding import PartitionSpec as P

SEG_LEN = 256
BINS = 32
FIRST_BIN = 2
ROWS = 2 * BINS
ALIGN = 16
LANES = 128
BAND = 2

EPS_POWER = 1e-06
MESH = pl.DeviceIdType.MESH
MIB = 1024 * 1024


def dft_tables(seg_length, bin_count, first_bin, shifts):
    sample_index = np.arange(seg_length)
    row_index = np.arange(2 * bin_count)
    harmonic = row_index // 2 + first_bin
    phase_steps = harmonic[:, None] * sample_index[None, :] % seg_length
    phase_angle = np.float32(2.0 * np.pi / seg_length) * phase_steps.astype(np.float32)
    taper_angle = np.float32(2.0 * np.pi / seg_length) * sample_index.astype(np.float32)
    hann_taper = np.float32(0.5) - np.float32(0.5) * np.cos(taper_angle)
    wave_rows = np.where((row_index % 2 == 0)[:, None], np.cos(phase_angle), -np.sin(phase_angle))
    table = (hann_taper[None, :] * wave_rows).astype(ml_dtypes.bfloat16)
    return np.stack([np.roll(table, m, axis=1) for m in range(shifts)], axis=0)


def whiten_kernel(offs_ref, x_ref, tab_ref, mask_ref, w_ref, flat_ref):
    seg_count = offs_ref.shape[0]
    cols = x_ref.shape[1]
    row = lax.broadcasted_iota(jnp.int32, (ALIGN, cols), 0)
    live = mask_ref[...].astype(jnp.float32)

    def segment(s, carry):
        start = offs_ref[s]
        m = lax.rem(start, ALIGN)
        base = pl.multiple_of(start - m, ALIGN)
        after = pl.multiple_of(jnp.minimum(base + SEG_LEN, x_ref.shape[0] - ALIGN), ALIGN)
        head = jnp.where(row >= m, x_ref[pl.ds(base, ALIGN), :], x_ref[pl.ds(after, ALIGN), :])
        body = x_ref[pl.ds(pl.multiple_of(base + ALIGN, ALIGN), SEG_LEN - ALIGN), :]
        frame = jnp.concatenate([head, body], axis=0)
        spectra = jnp.dot(tab_ref[m], frame, preferred_element_type=jnp.float32)
        power = jnp.sum(spectra * spectra, axis=0, keepdims=True) * (1.0 / BINS)
        scaled = spectra * (live / jnp.sqrt(power + EPS_POWER))
        for j in range(cols // LANES):
            flat_ref[j, pl.ds(s, ROWS, stride=seg_count), :] = scaled[:, j * LANES:(j + 1) * LANES]
        return carry

    lax.fori_loop(0, seg_count, segment, 0, unroll=2)

    def pack(r, carry):
        at = pl.ds(pl.multiple_of(r * seg_count, seg_count), seg_count)
        for j in range(cols // LANES):
            w_ref[r, :, j * LANES:(j + 1) * LANES] = flat_ref[j, at, :].astype(jnp.bfloat16)
        return carry

    lax.fori_loop(0, ROWS, pack, 0)


def whiten(records, offsets, dead_mask):
    seg_count = offsets.shape[0]
    cols = records.shape[1]
    tables = jnp.asarray(dft_tables(SEG_LEN, BINS, FIRST_BIN, ALIGN))
    vmem = pl.BlockSpec(memory_space=pltpu.VMEM)
    return pl.pallas_call(
        whiten_kernel,
        out_shape=jax.ShapeDtypeStruct((ROWS, seg_count, cols), jnp.bfloat16),
        in_specs=[pl.BlockSpec(memory_space=pltpu.SMEM), vmem, vmem, vmem],
        out_specs=vmem,
        scratch_shapes=[pltpu.VMEM((cols // LANES, ROWS * seg_count, LANES), jnp.float32)],
        compiler_params=pltpu.CompilerParams(vmem_limit_bytes=40 * MIB),
        cost_estimate=pl.CostEstimate(
            flops=2 * ROWS * SEG_LEN * cols * seg_count, bytes_accessed=13 * MIB, transcendentals=0
        ),
        name="whiten",
    )(offsets, records, tables, dead_mask.reshape(1, cols))


def peer_of(f, k):
    flipped = f
    bit = 1
    while bit <= k:
        if k & bit:
            flipped = flipped + bit - 2 * bit * ((f // bit) % 2)
        bit *= 2
    return flipped


def exchange_kernel(nchan, nfreq, chunks, w_ref, own_ref, up_ref, far_ref,
                    a_send, a_recv, z_send, z_recv, c_send, c_recv, l_sem):
    b = lax.axis_index("chan")
    f = lax.axis_index("freq")
    core = b % 2
    has_low = b >= 2
    has_high = b + 2 < nchan
    other = b + 1 - 2 * core
    per = own_ref.shape[1] // chunks

    barrier = pltpu.get_barrier_semaphore()
    for k in range(1, nfreq):
        pl.semaphore_signal(barrier, inc=1, device_id=(b, peer_of(f, k)), device_id_type=MESH)
    pl.semaphore_signal(barrier, inc=1, device_id=(other, f), device_id_type=MESH)

    @pl.when(has_low)
    def _():
        pl.semaphore_signal(barrier, inc=1, device_id=(b - 2, f), device_id_type=MESH)

    @pl.when(has_high)
    def _():
        pl.semaphore_signal(barrier, inc=1, device_id=(b + 2, f), device_id_type=MESH)

    greeted = nfreq + has_low.astype(jnp.int32) + has_high.astype(jnp.int32)
    pl.semaphore_wait(barrier, greeted)

    def rows(c):
        return pl.ds(c * per, per)

    def across(k, c):
        return pltpu.make_async_remote_copy(
            src_ref=w_ref.at[peer_of(f, k), rows(c)], dst_ref=own_ref.at[k, rows(c)],
            send_sem=a_send.at[k, c], recv_sem=a_recv.at[k, c],
            device_id=(b, peer_of(f, k)), device_id_type=MESH)

    def down(k, c):
        src = w_ref.at[f, rows(c)] if k == 0 else own_ref.at[k, rows(c)]
        return pltpu.make_async_remote_copy(
            src_ref=src, dst_ref=far_ref.at[k, rows(c)],
            send_sem=z_send.at[k, c], recv_sem=z_recv.at[k, c],
            device_id=(b - 2, f), device_id_type=MESH)

    def beside(src_ref, k, c):
        src = w_ref.at[f, rows(c)] if src_ref is None else src_ref.at[k, rows(c)]
        return pltpu.make_async_remote_copy(
            src_ref=src, dst_ref=up_ref.at[k, rows(c)],
            send_sem=c_send.at[k, c], recv_sem=c_recv.at[k, c],
            device_id=(other, f), device_id_type=MESH)

    for c in range(chunks):
        for k in range(1, nfreq):
            across(k, c).start()
    local = pltpu.make_async_copy(w_ref.at[f], own_ref.at[0], l_sem)
    local.start()

    for c in range(chunks):
        for k in range(nfreq):
            if k > 0:
                across(k, c).wait_recv()

            @pl.when(has_low)
            def _():
                down(k, c).start()

            @pl.when(core == 1)
            def _():
                beside(None if k == 0 else own_ref, k, c).start()

    for c in range(chunks):
        for k in range(nfreq):
            @pl.when(has_high)
            def _():
                down(k, c).wait_recv()

            @pl.when(has_high & (core == 0))
            def _():
                beside(far_ref, k, c).start()

    for c in range(chunks):
        for k in range(nfreq):
            if k > 0:
                across(k, c).wait_send()

            @pl.when(has_low)
            def _():
                down(k, c).wait_send()

            @pl.when(has_high | (core == 1))
            def _():
                beside(far_ref, k, c).wait_send()

            @pl.when(has_high | (core == 0))
            def _():
                beside(far_ref, k, c).wait_recv()

    local.wait()


def exchange(whitened, nchan, nfreq, chunks):
    _, seg_count, cols = whitened.shape
    mine = BINS // nfreq
    w = whitened.reshape(nfreq, mine, 2, seg_count, cols)
    panel = jax.ShapeDtypeStruct((nfreq, mine, 2, seg_count, cols), jnp.bfloat16)
    vmem = pl.BlockSpec(memory_space=pltpu.VMEM)
    pair = pltpu.SemaphoreType.DMA((nfreq, chunks))
    return pl.pallas_call(
        functools.partial(exchange_kernel, nchan, nfreq, chunks),
        out_shape=[panel] * 3,
        in_specs=[vmem],
        out_specs=[vmem] * 3,
        scratch_shapes=[pair] * 6 + [pltpu.SemaphoreType.DMA],
        compiler_params=pltpu.CompilerParams(
            collective_id=0, has_side_effects=True, vmem_limit_bytes=40 * MIB
        ),
        name="exchange",
    )(w)


def cross_kernel(keep_ref, own_ref, up_ref, far_ref, out_ref):
    nfreq, _, _, seg_count, cols = own_ref.shape
    depth = nfreq * 2 * seg_count
    scale = 1.0 / (nfreq * seg_count)
    left = own_ref[:, 0].reshape(depth, cols)
    turned = jnp.stack([own_ref[:, 0, 1], -own_ref[:, 0, 0]], axis=1).reshape(depth, cols)
    both = jnp.concatenate([left.T, turned.T], axis=0)
    for d, ref in enumerate((own_ref, up_ref, far_ref)):
        @pl.when(keep_ref[d] != 0)
        def _():
            right = ref[:, 0].reshape(depth, cols)
            product = jnp.dot(both, right, preferred_element_type=jnp.float32) * scale
            out_ref[d, 0, :, :cols] = product[:cols].astype(jnp.bfloat16)
            out_ref[d, 0, :, cols:] = product[cols:].astype(jnp.bfloat16)

        @pl.when(keep_ref[d] == 0)
        def _():
            out_ref[d] = jnp.zeros(out_ref.shape[1:], jnp.bfloat16)


def cross(keep, own, up, far):
    nfreq, mine, _, seg_count, cols = own.shape
    panel = pl.BlockSpec((nfreq, 1, 2, seg_count, cols), lambda i: (0, i, 0, 0, 0))
    return pl.pallas_call(
        cross_kernel,
        grid=(mine,),
        out_shape=jax.ShapeDtypeStruct((BAND + 1, mine, cols, 2 * cols), jnp.bfloat16),
        in_specs=[pl.BlockSpec(memory_space=pltpu.SMEM), panel, panel, panel],
        out_specs=pl.BlockSpec((BAND + 1, 1, cols, 2 * cols), lambda i: (0, i, 0, 0)),
        compiler_params=pltpu.CompilerParams(vmem_limit_bytes=40 * MIB),
        cost_estimate=pl.CostEstimate(
            flops=12 * mine * cols * cols * 2 * nfreq * seg_count, bytes_accessed=40 * MIB, transcendentals=0
        ),
        name="cross",
    )(keep, own, up, far)


def shards(nchan, nfreq, records, offsets, dead_mask, band_blocks):
    whitened = whiten(records, offsets, dead_mask)
    own, up, far = exchange(whitened, nchan, nfreq, 4)
    b = lax.axis_index("chan")
    offset = jnp.arange(BAND + 1, dtype=jnp.int32)
    keep = ((offset <= band_blocks[0]) & (b + offset < nchan)).astype(jnp.int32)
    return cross(keep, own, up, far)


def solution(mesh):
    in_specs = (P("freq", "chan"), P("freq"), P("chan"), P("chan"))
    out_specs = P(None, "freq", "chan", None)
    body = functools.partial(shards, mesh.shape["chan"], mesh.shape["freq"])
    return jax.shard_map(body, mesh=mesh, in_specs=in_specs, out_specs=out_specs, check_vma=False)
```

```python
import functools

import jax
import jax.numpy as jnp
import ml_dtypes
import numpy as np
from jax import lax
from jax.experimental import pallas as pl
from jax.experimental.pallas import tpu as pltpu
from jax.sharding import PartitionSpec as P

SEG_LEN = 256
BINS = 32
FIRST_BIN = 2
ROWS = 2 * BINS
ALIGN = 16
LANES = 128
GROUP = 16
CHUNKS = 4
BAND = 2

EPS_POWER = 1e-06
MESH = pl.DeviceIdType.MESH
MIB = 1024 * 1024


def dft_tables(seg_length, bin_count, first_bin, shifts):
    sample_index = np.arange(seg_length)
    row_index = np.arange(2 * bin_count)
    harmonic = row_index // 2 + first_bin
    phase_steps = harmonic[:, None] * sample_index[None, :] % seg_length
    phase_angle = np.float32(2.0 * np.pi / seg_length) * phase_steps.astype(np.float32)
    taper_angle = np.float32(2.0 * np.pi / seg_length) * sample_index.astype(np.float32)
    hann_taper = np.float32(0.5) - np.float32(0.5) * np.cos(taper_angle)
    wave_rows = np.where((row_index % 2 == 0)[:, None], np.cos(phase_angle), -np.sin(phase_angle))
    table = (hann_taper[None, :] * wave_rows).astype(ml_dtypes.bfloat16)
    return np.stack([np.roll(table, m, axis=1) for m in range(shifts)], axis=0)


def whiten_kernel(offs_ref, x_ref, tab_ref, mask_ref, w_ref, flat_ref):
    seg_count = offs_ref.shape[0]
    cols = x_ref.shape[1]
    row = lax.broadcasted_iota(jnp.int32, (ALIGN, cols), 0)
    live = mask_ref[...].astype(jnp.float32)

    def whiten_group(g, carry):
        def segment(s, carry):
            start = offs_ref[g * GROUP + s]
            m = start % ALIGN
            base = pl.multiple_of(start - m, ALIGN)
            after = pl.multiple_of(jnp.minimum(base + SEG_LEN, x_ref.shape[0] - ALIGN), ALIGN)
            head = jnp.where(row >= m, x_ref[pl.ds(base, ALIGN), :], x_ref[pl.ds(after, ALIGN), :])
            body = x_ref[pl.ds(pl.multiple_of(base + ALIGN, ALIGN), SEG_LEN - ALIGN), :]
            frame = jnp.concatenate([head, body], axis=0)
            spectra = jnp.dot(tab_ref[m], frame, preferred_element_type=jnp.float32)
            power = jnp.sum(spectra * spectra, axis=0, keepdims=True) * (1.0 / BINS)
            scaled = spectra * (live * lax.rsqrt(power + EPS_POWER))
            for j in range(cols // LANES):
                flat_ref[j, pl.ds(s, ROWS, stride=GROUP), :] = scaled[:, j * LANES:(j + 1) * LANES]
            return carry

        lax.fori_loop(0, GROUP, segment, 0, unroll=4)

        def pack(r, carry):
            at = pl.ds(pl.multiple_of(r * GROUP, GROUP), GROUP)
            for j in range(cols // LANES):
                w_ref[r, pl.ds(pl.multiple_of(g * GROUP, GROUP), GROUP), j * LANES:(j + 1) * LANES] = flat_ref[j, at, :].astype(jnp.bfloat16)
            return carry

        lax.fori_loop(0, ROWS, pack, 0, unroll=4)
        return carry

    lax.fori_loop(0, seg_count // GROUP, whiten_group, 0)


def whiten(records, offsets, dead_mask):
    seg_count = offsets.shape[0]
    cols = records.shape[1]
    tables = jnp.asarray(dft_tables(SEG_LEN, BINS, FIRST_BIN, ALIGN))
    vmem = pl.BlockSpec(memory_space=pltpu.VMEM)
    return pl.pallas_call(
        whiten_kernel,
        out_shape=jax.ShapeDtypeStruct((ROWS, seg_count, cols), jnp.bfloat16),
        in_specs=[pl.BlockSpec(memory_space=pltpu.SMEM), vmem, vmem, vmem],
        out_specs=vmem,
        scratch_shapes=[pltpu.VMEM((cols // LANES, ROWS * GROUP, LANES), jnp.float32)],
        compiler_params=pltpu.CompilerParams(vmem_limit_bytes=24 * MIB),
        cost_estimate=pl.CostEstimate(
            flops=2 * ROWS * SEG_LEN * cols * seg_count, bytes_accessed=13 * MIB, transcendentals=0
        ),
        name="whiten",
    )(offsets, records, tables, dead_mask.reshape(1, cols))


def peer_of(f, k):
    flipped = f
    bit = 1
    while bit <= k:
        if k & bit:
            flipped = flipped + bit - 2 * bit * ((f // bit) % 2)
        bit *= 2
    return flipped


def product(own_ref, right_ref, i, out_ref, *at):
    nfreq, _, seg_count, cols = own_ref.shape
    depth = nfreq * 2 * seg_count
    scale = 1.0 / (nfreq * seg_count)
    pair = own_ref[:, pl.ds(2 * i, 2)]
    left = pair.reshape(depth, cols)
    turned = jnp.stack([pair[:, 1], -pair[:, 0]], axis=1).reshape(depth, cols)
    both = jnp.concatenate([left.T, turned.T], axis=0)
    right = right_ref[:, pl.ds(2 * i, 2)].reshape(depth, cols)
    result = jnp.dot(both, right, preferred_element_type=jnp.float32) * scale
    out_ref[(*at, slice(None), slice(0, cols))] = result[:cols].astype(jnp.bfloat16)
    out_ref[(*at, slice(None), slice(cols, 2 * cols))] = result[cols:].astype(jnp.bfloat16)


def exchange_kernel(nchan, nfreq, chunks, w_ref,
                    own_ref, up_ref, far_ref, first_ref, second_ref, third_ref,
                    a_send, a_recv, z_send, z_recv, c_send, c_recv,
                    z0_send, z0_recv, c0_send, c0_recv, l_sem):
    b = lax.axis_index("chan")
    f = lax.axis_index("freq")
    core = b % 2
    has_low = b >= 2
    has_high = b + 2 < nchan
    has_up = has_high | (core == 0)
    other = b + 1 - 2 * core
    mine = own_ref.shape[1]
    seg_count, cols = w_ref.shape[1:]
    per = mine // chunks

    barrier = pltpu.get_barrier_semaphore()
    for k in range(1, nfreq):
        pl.semaphore_signal(barrier, inc=1, device_id=(b, peer_of(f, k)), device_id_type=MESH)
    pl.semaphore_signal(barrier, inc=1, device_id=(other, f), device_id_type=MESH)

    @pl.when(has_low)
    def _():
        pl.semaphore_signal(barrier, inc=1, device_id=(b - 2, f), device_id_type=MESH)

    @pl.when(has_high)
    def _():
        pl.semaphore_signal(barrier, inc=1, device_id=(b + 2, f), device_id_type=MESH)

    greeted = nfreq + has_low.astype(jnp.int32) + has_high.astype(jnp.int32)
    pl.semaphore_wait(barrier, greeted)

    def bins_of(device, c):
        return pl.ds(device * mine + c * per, per)

    def rows(c):
        return pl.ds(c * per, per)

    def across(k, c):
        return pltpu.make_async_remote_copy(
            src_ref=w_ref.at[bins_of(peer_of(f, k), c)], dst_ref=own_ref.at[k, rows(c)],
            send_sem=a_send.at[k, c], recv_sem=a_recv.at[k, c],
            device_id=(b, peer_of(f, k)), device_id_type=MESH)

    def down(k, c):
        return pltpu.make_async_remote_copy(
            src_ref=own_ref.at[k, rows(c)], dst_ref=far_ref.at[k, rows(c)],
            send_sem=z_send.at[k, c], recv_sem=z_recv.at[k, c],
            device_id=(b - 2, f), device_id_type=MESH)

    def beside(src_ref, k, c):
        return pltpu.make_async_remote_copy(
            src_ref=src_ref.at[k, rows(c)], dst_ref=up_ref.at[k, rows(c)],
            send_sem=c_send.at[k, c], recv_sem=c_recv.at[k, c],
            device_id=(other, f), device_id_type=MESH)

    down0 = pltpu.make_async_remote_copy(
        src_ref=w_ref.at[pl.ds(f * mine, mine)], dst_ref=far_ref.at[0],
        send_sem=z0_send, recv_sem=z0_recv,
        device_id=(b - 2, f), device_id_type=MESH)

    def beside0(passed):
        return pltpu.make_async_remote_copy(
            src_ref=far_ref.at[0] if passed else w_ref.at[pl.ds(f * mine, mine)], dst_ref=up_ref.at[0],
            send_sem=c0_send, recv_sem=c0_recv,
            device_id=(other, f), device_id_type=MESH)

    @pl.when(has_low)
    def _():
        down0.start()

    @pl.when(core == 1)
    def _():
        beside0(False).start()

    for c in range(chunks):
        for k in range(1, nfreq):
            across(k, c).start()
    local = pltpu.make_async_copy(w_ref.at[pl.ds(f * mine, mine)], own_ref.at[0], l_sem)
    local.start()
    local.wait()

    def own_chunk(c, carry):
        for k in range(1, nfreq):
            across(k, c).wait_recv()

            @pl.when(has_low)
            def _():
                down(k, c).start()

            @pl.when(core == 1)
            def _():
                beside(own_ref, k, c).start()

        def one_bin(j, inner):
            i = c * (per // 2) + j
            product(own_ref, own_ref, i, first_ref, i)
            return inner

        lax.fori_loop(0, per // 2, one_bin, 0)
        return carry

    lax.fori_loop(0, chunks, own_chunk, 0)

    @pl.when(has_high)
    def _():
        down0.wait_recv()

    @pl.when(has_high & (core == 0))
    def _():
        beside0(True).start()

    @pl.when(has_up)
    def _():
        beside0(True).wait_recv()

    def far_chunk(c, carry):
        for k in range(1, nfreq):
            @pl.when(has_high)
            def _():
                down(k, c).wait_recv()

            @pl.when(has_high & (core == 0))
            def _():
                beside(far_ref, k, c).start()

        for k in range(1, nfreq):
            @pl.when(has_up)
            def _():
                beside(far_ref, k, c).wait_recv()

        def one_bin(j, inner):
            i = c * (per // 2) + j

            @pl.when(has_up)
            def _():
                product(own_ref, up_ref, i, second_ref, i)

            @pl.when(has_high)
            def _():
                product(own_ref, far_ref, i, third_ref, i)

            return inner

        @pl.when(c < chunks - 1)
        def _():
            lax.fori_loop(0, per // 2, one_bin, 0)

        return carry

    lax.fori_loop(0, chunks, far_chunk, 0)

    def settle(c, carry):
        for k in range(1, nfreq):
            across(k, c).wait_send()

            @pl.when(has_low)
            def _():
                down(k, c).wait_send()

            @pl.when(has_high | (core == 1))
            def _():
                beside(far_ref, k, c).wait_send()

        return carry

    lax.fori_loop(0, chunks, settle, 0)

    @pl.when(has_low)
    def _():
        down0.wait_send()

    @pl.when(has_high | (core == 1))
    def _():
        beside0(True).wait_send()


def exchange(whitened, nchan, nfreq):
    _, seg_count, cols = whitened.shape
    mine = ROWS // nfreq
    chunks = CHUNKS
    panel = jax.ShapeDtypeStruct((nfreq, mine, seg_count, cols), jnp.bfloat16)
    bins = mine // 2
    ahead = bins - bins // chunks
    results = [jax.ShapeDtypeStruct((n, cols, 2 * cols), jnp.bfloat16) for n in (bins, ahead, ahead)]
    vmem = pl.BlockSpec(memory_space=pltpu.VMEM)
    pair = pltpu.SemaphoreType.DMA((nfreq, chunks))
    return pl.pallas_call(
        functools.partial(exchange_kernel, nchan, nfreq, chunks),
        out_shape=[panel] * 3 + results,
        in_specs=[vmem],
        out_specs=[vmem] * 6,
        scratch_shapes=[pair] * 6 + [pltpu.SemaphoreType.DMA] * 5,
        compiler_params=pltpu.CompilerParams(
            collective_id=0, has_side_effects=True, vmem_limit_bytes=10 * MIB
        ),
        name="exchange",
    )(whitened)


def cross_kernel(keep_ref, own_ref, up_ref, far_ref, first_ref, second_ref, third_ref, out_ref):
    i = pl.program_id(0)
    done = ((own_ref, first_ref), (up_ref, second_ref), (far_ref, third_ref))
    for d, (right_ref, ahead_ref) in enumerate(done):
        count = ahead_ref.shape[0]

        @pl.when((keep_ref[d] != 0) & (i < count))
        def _():
            out_ref[d, 0] = ahead_ref[jnp.minimum(i, count - 1)]

        if count < first_ref.shape[0]:
            @pl.when((keep_ref[d] != 0) & (i >= count))
            def _():
                product(own_ref, right_ref, i, out_ref, d, 0)

        @pl.when(keep_ref[d] == 0)
        def _():
            out_ref[d] = jnp.zeros(out_ref.shape[1:], jnp.bfloat16)


def cross(keep, *parts):
    nfreq, mine, seg_count, cols = parts[0].shape
    bins = mine // 2
    vmem = pl.BlockSpec(memory_space=pltpu.VMEM)
    return pl.pallas_call(
        cross_kernel,
        grid=(bins,),
        out_shape=jax.ShapeDtypeStruct((BAND + 1, bins, cols, 2 * cols), jnp.bfloat16),
        in_specs=[pl.BlockSpec(memory_space=pltpu.SMEM)] + [vmem] * 6,
        out_specs=pl.BlockSpec((BAND + 1, 1, cols, 2 * cols), lambda i: (0, i, 0, 0)),
        compiler_params=pltpu.CompilerParams(vmem_limit_bytes=15 * MIB),
        cost_estimate=pl.CostEstimate(
            flops=3 * bins * cols * cols * 2 * nfreq * seg_count, bytes_accessed=26 * MIB, transcendentals=0
        ),
        name="cross",
    )(keep, *parts)


def shards(nchan, nfreq, records, offsets, dead_mask, band_blocks):
    parts = exchange(whiten(records, offsets, dead_mask), nchan, nfreq)
    b = lax.axis_index("chan")
    offset = jnp.arange(BAND + 1, dtype=jnp.int32)
    keep = ((offset <= band_blocks[0]) & (b + offset < nchan)).astype(jnp.int32)
    return cross(keep, *parts)


def solution(mesh):
    in_specs = (P("freq", "chan"), P("freq"), P("chan"), P("chan"))
    out_specs = P(None, "freq", "chan", None)
    body = functools.partial(shards, mesh.shape["chan"], mesh.shape["freq"])
    return jax.shard_map(body, mesh=mesh, in_specs=in_specs, out_specs=out_specs, check_vma=False)
```

```python
import functools

import jax
import jax.numpy as jnp
import ml_dtypes
import numpy as np
from jax import lax
from jax.experimental import pallas as pl
from jax.experimental.pallas import tpu as pltpu
from jax.sharding import PartitionSpec as P

SEG_LEN = 256
BINS = 32
FIRST_BIN = 2
ROWS = 2 * BINS
ALIGN = 16
LANES = 128
GROUP = 16
BAND = 2

EPS_POWER = 1e-06
MESH = pl.DeviceIdType.MESH
MIB = 1024 * 1024


def dft_tables(seg_length, bin_count, first_bin, shifts):
    sample_index = np.arange(seg_length)
    row_index = np.arange(2 * bin_count)
    harmonic = row_index // 2 + first_bin
    phase_steps = harmonic[:, None] * sample_index[None, :] % seg_length
    phase_angle = np.float32(2.0 * np.pi / seg_length) * phase_steps.astype(np.float32)
    taper_angle = np.float32(2.0 * np.pi / seg_length) * sample_index.astype(np.float32)
    hann_taper = np.float32(0.5) - np.float32(0.5) * np.cos(taper_angle)
    wave_rows = np.where((row_index % 2 == 0)[:, None], np.cos(phase_angle), -np.sin(phase_angle))
    table = (hann_taper[None, :] * wave_rows).astype(ml_dtypes.bfloat16)
    return np.stack([np.roll(table, m, axis=1) for m in range(shifts)], axis=0)


def whiten_kernel(offs_ref, x_ref, tab_ref, mask_ref, w_ref, flat_ref):
    seg_count = offs_ref.shape[0]
    cols = x_ref.shape[1]
    row = lax.broadcasted_iota(jnp.int32, (ALIGN, cols), 0)
    live = mask_ref[...].astype(jnp.float32)

    def whiten_group(g, carry):
        def segment(s, carry):
            start = offs_ref[g * GROUP + s]
            m = start % ALIGN
            base = pl.multiple_of(start - m, ALIGN)
            after = pl.multiple_of(jnp.minimum(base + SEG_LEN, x_ref.shape[0] - ALIGN), ALIGN)
            head = jnp.where(row >= m, x_ref[pl.ds(base, ALIGN), :], x_ref[pl.ds(after, ALIGN), :])
            body = x_ref[pl.ds(pl.multiple_of(base + ALIGN, ALIGN), SEG_LEN - ALIGN), :]
            frame = jnp.concatenate([head, body], axis=0)
            spectra = jnp.dot(tab_ref[m], frame, preferred_element_type=jnp.float32)
            power = jnp.sum(spectra * spectra, axis=0, keepdims=True) * (1.0 / BINS)
            scaled = spectra * (live * lax.rsqrt(power + EPS_POWER))
            for j in range(cols // LANES):
                flat_ref[j, pl.ds(s, ROWS, stride=GROUP), :] = scaled[:, j * LANES:(j + 1) * LANES]
            return carry

        lax.fori_loop(0, GROUP, segment, 0, unroll=8)

        def pack(r, carry):
            at = pl.ds(pl.multiple_of(r * GROUP, GROUP), GROUP)
            for j in range(cols // LANES):
                w_ref[r, pl.ds(pl.multiple_of(g * GROUP, GROUP), GROUP), j * LANES:(j + 1) * LANES] = flat_ref[j, at, :].astype(jnp.bfloat16)
            return carry

        lax.fori_loop(0, ROWS, pack, 0, unroll=4)
        return carry

    lax.fori_loop(0, seg_count // GROUP, whiten_group, 0)


def whiten(records, offsets, dead_mask):
    seg_count = offsets.shape[0]
    cols = records.shape[1]
    tables = jnp.asarray(dft_tables(SEG_LEN, BINS, FIRST_BIN, ALIGN))
    vmem = pl.BlockSpec(memory_space=pltpu.VMEM)
    return pl.pallas_call(
        whiten_kernel,
        out_shape=jax.ShapeDtypeStruct((ROWS, seg_count, cols), jnp.bfloat16),
        in_specs=[pl.BlockSpec(memory_space=pltpu.SMEM), vmem, vmem, vmem],
        out_specs=vmem,
        scratch_shapes=[pltpu.VMEM((cols // LANES, ROWS * GROUP, LANES), jnp.float32)],
        compiler_params=pltpu.CompilerParams(vmem_limit_bytes=24 * MIB),
        cost_estimate=pl.CostEstimate(
            flops=2 * ROWS * SEG_LEN * cols * seg_count, bytes_accessed=13 * MIB, transcendentals=0
        ),
        name="whiten",
    )(offsets, records, tables, dead_mask.reshape(1, cols))


def peer_of(f, k):
    flipped = f
    bit = 1
    while bit <= k:
        if k & bit:
            flipped = flipped + bit - 2 * bit * ((f // bit) % 2)
        bit *= 2
    return flipped


def product(own_ref, right_ref, i, out_ref, *at):
    nfreq, _, seg_count, cols = own_ref.shape
    depth = nfreq * 2 * seg_count
    scale = 1.0 / (nfreq * seg_count)
    pair = own_ref[:, pl.ds(2 * i, 2)]
    left = pair.reshape(depth, cols)
    turned = jnp.stack([pair[:, 1], -pair[:, 0]], axis=1).reshape(depth, cols)
    both = jnp.concatenate([left.T, turned.T], axis=0)
    right = right_ref[:, pl.ds(2 * i, 2)].reshape(depth, cols)
    result = jnp.dot(both, right, preferred_element_type=jnp.float32) * scale
    out_ref[(*at, slice(None), slice(0, cols))] = result[:cols].astype(jnp.bfloat16)
    out_ref[(*at, slice(None), slice(cols, 2 * cols))] = result[cols:].astype(jnp.bfloat16)


def exchange_kernel(nchan, nfreq, chunks, w_ref,
                    own_ref, up_ref, far_ref, first_ref, second_ref, third_ref,
                    a_send, a_recv, z_send, z_recv, c_send, c_recv,
                    z0_send, z0_recv, c0_send, c0_recv, l_sem):
    b = lax.axis_index("chan")
    f = lax.axis_index("freq")
    core = b % 2
    has_low = b >= 2
    has_high = b + 2 < nchan
    has_up = has_high | (core == 0)
    other = b + 1 - 2 * core
    mine = own_ref.shape[1]
    seg_count, cols = w_ref.shape[1:]
    per = mine // chunks

    barrier = pltpu.get_barrier_semaphore()
    for k in range(1, nfreq):
        pl.semaphore_signal(barrier, inc=1, device_id=(b, peer_of(f, k)), device_id_type=MESH)
    pl.semaphore_signal(barrier, inc=1, device_id=(other, f), device_id_type=MESH)

    @pl.when(has_low)
    def _():
        pl.semaphore_signal(barrier, inc=1, device_id=(b - 2, f), device_id_type=MESH)

    @pl.when(has_high)
    def _():
        pl.semaphore_signal(barrier, inc=1, device_id=(b + 2, f), device_id_type=MESH)

    greeted = nfreq + has_low.astype(jnp.int32) + has_high.astype(jnp.int32)
    pl.semaphore_wait(barrier, greeted)

    def bins_of(device, c):
        return pl.ds(device * mine + c * per, per)

    def rows(c):
        return pl.ds(c * per, per)

    def across(k, c):
        return pltpu.make_async_remote_copy(
            src_ref=w_ref.at[bins_of(peer_of(f, k), c)], dst_ref=own_ref.at[k, rows(c)],
            send_sem=a_send.at[k, c], recv_sem=a_recv.at[k, c],
            device_id=(b, peer_of(f, k)), device_id_type=MESH)

    def down(k, c):
        return pltpu.make_async_remote_copy(
            src_ref=own_ref.at[k, rows(c)], dst_ref=far_ref.at[k, rows(c)],
            send_sem=z_send.at[k, c], recv_sem=z_recv.at[k, c],
            device_id=(b - 2, f), device_id_type=MESH)

    def beside(src_ref, k, c):
        return pltpu.make_async_remote_copy(
            src_ref=src_ref.at[k, rows(c)], dst_ref=up_ref.at[k, rows(c)],
            send_sem=c_send.at[k, c], recv_sem=c_recv.at[k, c],
            device_id=(other, f), device_id_type=MESH)

    down0 = pltpu.make_async_remote_copy(
        src_ref=w_ref.at[pl.ds(f * mine, mine)], dst_ref=far_ref.at[0],
        send_sem=z0_send, recv_sem=z0_recv,
        device_id=(b - 2, f), device_id_type=MESH)

    def beside0(passed):
        return pltpu.make_async_remote_copy(
            src_ref=far_ref.at[0] if passed else w_ref.at[pl.ds(f * mine, mine)], dst_ref=up_ref.at[0],
            send_sem=c0_send, recv_sem=c0_recv,
            device_id=(other, f), device_id_type=MESH)

    @pl.when(has_low)
    def _():
        down0.start()

    @pl.when(core == 1)
    def _():
        beside0(False).start()

    for c in range(chunks):
        for k in range(1, nfreq):
            across(k, c).start()
    local = pltpu.make_async_copy(w_ref.at[pl.ds(f * mine, mine)], own_ref.at[0], l_sem)
    local.start()
    local.wait()

    def own_chunk(c, carry):
        for k in range(1, nfreq):
            across(k, c).wait_recv()

            @pl.when(has_low)
            def _():
                down(k, c).start()

            @pl.when(core == 1)
            def _():
                beside(own_ref, k, c).start()

        def one_bin(j, inner):
            i = c * (per // 2) + j
            product(own_ref, own_ref, i, first_ref, i)
            return inner

        lax.fori_loop(0, per // 2, one_bin, 0)
        return carry

    lax.fori_loop(0, chunks, own_chunk, 0)

    @pl.when(has_high)
    def _():
        down0.wait_recv()

    @pl.when(has_high & (core == 0))
    def _():
        beside0(True).start()

    @pl.when(has_up)
    def _():
        beside0(True).wait_recv()

    def far_chunk(c, carry):
        for k in range(1, nfreq):
            @pl.when(has_high)
            def _():
                down(k, c).wait_recv()

            @pl.when(has_high & (core == 0))
            def _():
                beside(far_ref, k, c).start()

        for k in range(1, nfreq):
            @pl.when(has_up)
            def _():
                beside(far_ref, k, c).wait_recv()

        def one_bin(j, inner):
            i = c * (per // 2) + j

            @pl.when(has_up)
            def _():
                product(own_ref, up_ref, i, second_ref, i)

            @pl.when(has_high)
            def _():
                product(own_ref, far_ref, i, third_ref, i)

            return inner

        @pl.when(c < chunks - 1)
        def _():
            lax.fori_loop(0, per // 2, one_bin, 0)

        return carry

    lax.fori_loop(0, chunks, far_chunk, 0)

    def settle(c, carry):
        for k in range(1, nfreq):
            across(k, c).wait_send()

            @pl.when(has_low)
            def _():
                down(k, c).wait_send()

            @pl.when(has_high | (core == 1))
            def _():
                beside(far_ref, k, c).wait_send()

        return carry

    lax.fori_loop(0, chunks, settle, 0)

    @pl.when(has_low)
    def _():
        down0.wait_send()

    @pl.when(has_high | (core == 1))
    def _():
        beside0(True).wait_send()


def exchange(whitened, nchan, nfreq):
    _, seg_count, cols = whitened.shape
    mine = ROWS // nfreq
    chunks = mine // 2
    panel = jax.ShapeDtypeStruct((nfreq, mine, seg_count, cols), jnp.bfloat16)
    bins = mine // 2
    ahead = bins - bins // chunks
    results = [jax.ShapeDtypeStruct((n, cols, 2 * cols), jnp.bfloat16) for n in (bins, ahead, ahead)]
    vmem = pl.BlockSpec(memory_space=pltpu.VMEM)
    pair = pltpu.SemaphoreType.DMA((nfreq, chunks))
    return pl.pallas_call(
        functools.partial(exchange_kernel, nchan, nfreq, chunks),
        out_shape=[panel] * 3 + results,
        in_specs=[vmem],
        out_specs=[vmem] * 6,
        scratch_shapes=[pair] * 6 + [pltpu.SemaphoreType.DMA] * 5,
        compiler_params=pltpu.CompilerParams(
            collective_id=0, has_side_effects=True, vmem_limit_bytes=10 * MIB
        ),
        name="exchange",
    )(whitened)


def cross_kernel(keep_ref, own_ref, up_ref, far_ref, first_ref, second_ref, third_ref, out_ref):
    i = pl.program_id(0)
    done = ((own_ref, first_ref), (up_ref, second_ref), (far_ref, third_ref))
    for d, (right_ref, ahead_ref) in enumerate(done):
        count = ahead_ref.shape[0]

        @pl.when((keep_ref[d] != 0) & (i < count))
        def _():
            out_ref[d, 0] = ahead_ref[jnp.minimum(i, count - 1)]

        if count < first_ref.shape[0]:
            @pl.when((keep_ref[d] != 0) & (i >= count))
            def _():
                product(own_ref, right_ref, i, out_ref, d, 0)

        @pl.when(keep_ref[d] == 0)
        def _():
            out_ref[d] = jnp.zeros(out_ref.shape[1:], jnp.bfloat16)


def cross(keep, *parts):
    nfreq, mine, seg_count, cols = parts[0].shape
    bins = mine // 2
    vmem = pl.BlockSpec(memory_space=pltpu.VMEM)
    return pl.pallas_call(
        cross_kernel,
        grid=(bins,),
        out_shape=jax.ShapeDtypeStruct((BAND + 1, bins, cols, 2 * cols), jnp.bfloat16),
        in_specs=[pl.BlockSpec(memory_space=pltpu.SMEM)] + [vmem] * 6,
        out_specs=pl.BlockSpec((BAND + 1, 1, cols, 2 * cols), lambda i: (0, i, 0, 0)),
        compiler_params=pltpu.CompilerParams(vmem_limit_bytes=15 * MIB),
        cost_estimate=pl.CostEstimate(
            flops=3 * bins * cols * cols * 2 * nfreq * seg_count, bytes_accessed=26 * MIB, transcendentals=0
        ),
        name="cross",
    )(keep, *parts)


def shards(nchan, nfreq, records, offsets, dead_mask, band_blocks):
    parts = exchange(whiten(records, offsets, dead_mask), nchan, nfreq)
    b = lax.axis_index("chan")
    offset = jnp.arange(BAND + 1, dtype=jnp.int32)
    keep = ((offset <= band_blocks[0]) & (b + offset < nchan)).astype(jnp.int32)
    return cross(keep, *parts)


def solution(mesh):
    in_specs = (P("freq", "chan"), P("freq"), P("chan"), P("chan"))
    out_specs = P(None, "freq", "chan", None)
    body = functools.partial(shards, mesh.shape["chan"], mesh.shape["freq"])
    return jax.shard_map(body, mesh=mesh, in_specs=in_specs, out_specs=out_specs, check_vma=False)
```
